32 devices in a mesh: group: 2 (over x), expert: 4 (over y, core), dp: 4 (over z).
Axes of the slice: x: 2, y: 2, z: 4, core: 2. Of those that a mesh axis runs over, the one named last changes fastest.
Arguments:
- tokens: bfloat16 [1024, 7168], P(('group', 'expert', 'dp')), parts along dimension 0, may hold values from -6 to 6
- affinity: float32 [1024, 8], P(('group', 'expert', 'dp')), parts along dimension 0, may hold values from 0.05 to 1
- expert_ids: int32 [1024, 8], P(('group', 'expert', 'dp')), parts along dimension 0, may hold values from 0 to 255, as said below
- swap_partner: int32 [8], P('group'), parts along dimension 0, may hold values from 0 to 3, as said below
- gate_up: bfloat16 [4, 2, 7168, 1024], P('expert', None, None, 'dp'), may hold values from -6 to 6
- down_proj: bfloat16 [4, 1024, 7168], P('expert', 'dp'), may hold values from -6 to 6
Outputs:
- moe_out: bfloat16 [1024, 7168], P(('group', 'expert', 'dp')), parts along dimension 0
- new_gate_up: bfloat16 [8, 2, 7168, 1024], P(('group', 'expert'), None, None, 'dp'), parts along dimension 0
- new_down: bfloat16 [8, 1024, 7168], P(('group', 'expert'), 'dp'), parts along dimension 0
The draws below stay inside these ranges and needn't reach their ends.
There are 2 independent parts, one for each index of `group`. The reference program is written for one: setup_inputs(seed, part) draws one part's arguments, and reference() takes and returns one part's arrays. A program takes and returns all parts, laid end to end along the dimension named above; an argument that names none is the same for every part. Nothing has to cross between parts.
Inputs may be any that keep to these rules, and one draw needn't show every extreme that they name: `expert_ids`: each row names 8 different experts. In each aligned block of 32 rows (the rows of one device), each expert below 4 is named by at most 2 rows, and one expert below 4 is named by exactly 2 rows in every block. swap_partner[e] is e or the slot 2 away from e (e + 4 / 2 modulo 4), swap_partner[swap_partner[e]] = e, and at least one pair of slots swaps.
All inputs are finite; a program needn't handle non-finite values.
Results may differ from the reference program's by a relative error of at most 0.009.
Values may be sent and summed in bfloat16 or wider, within the bound.
A program may use at most 64 MiB of HBM per device.

```python
import math
import jax
import jax.numpy as jnp
from jax import lax

D = 7168
HID = 1024
EXPERTS_ALL = 256
TOP = 8
TOK_DEV = 32
CAP = 2
TOKENS = 512
N_EXPERT = 4
N_DP = 4


def block_ids(block_key, hot_expert):
    key_order = jax.random.fold_in(block_key, 1)
    key_counts = jax.random.fold_in(block_key, 2)
    key_base = jax.random.fold_in(block_key, 3)
    key_stride = jax.random.fold_in(block_key, 4)
    key_roll = jax.random.fold_in(block_key, 5)
    order = jax.random.permutation(key_order, TOK_DEV).astype(jnp.int32)
    counts = jax.random.randint(key_counts, (N_EXPERT,), 0, CAP + 1)
    counts = jnp.where(jnp.arange(N_EXPERT) == hot_expert, CAP, counts)
    places = jnp.arange(N_EXPERT * CAP)
    expert_of = places // CAP
    used = (places % CAP < counts[expert_of]).astype(jnp.int32)
    token_of = order[places % TOK_DEV]
    chosen = jnp.zeros((TOK_DEV, N_EXPERT), jnp.int32).at[token_of, expert_of].max(used)
    inside_count = jnp.sum(chosen, axis=1)
    rank_table = jnp.cumsum(chosen, axis=1) - chosen
    place = jnp.arange(TOP)
    expert_range = jnp.arange(N_EXPERT)
    hits = chosen[:, None, :] * (rank_table[:, None, :] == place[None, :, None]).astype(jnp.int32)
    window_id = jnp.sum(hits * expert_range[None, None, :], axis=2)
    span = EXPERTS_ALL - N_EXPERT
    base = jax.random.randint(key_base, (TOK_DEV, 1), 0, span)
    stride = jax.random.randint(key_stride, (TOK_DEV, 1), 1, span // TOP + 1)
    outer_id = N_EXPERT + (base + (place[None, :] - inside_count[:, None]) * stride) % span
    row = jnp.where(place[None, :] < inside_count[:, None], window_id, outer_id)
    shift = jax.random.randint(key_roll, (TOK_DEV, 1), 0, TOP)
    row = jnp.take_along_axis(row, (place[None, :] + shift) % TOP, axis=1)
    return row.astype(jnp.int32)


def draw_expert_ids(key, part):
    n_blocks = TOKENS // TOK_DEV
    hot_expert = jax.random.randint(jax.random.fold_in(key, 7), (), 0, N_EXPERT)
    block_keys = jax.random.split(jax.random.fold_in(key, 11), n_blocks)
    rows = jax.vmap(lambda block_key: block_ids(block_key, hot_expert))(block_keys)
    return rows.reshape(TOKENS, TOP).astype(jnp.int32)


def draw_swap_partner(key, part):
    half = N_EXPERT // 2
    flags = jax.random.randint(jax.random.fold_in(key, 21), (half,), 0, 2)
    forced = jax.random.randint(jax.random.fold_in(key, 23), (), 0, half)
    flags = jnp.where(jnp.arange(half) == forced, 1, flags)
    slots_all = jnp.arange(N_EXPERT)
    paired = jnp.concatenate([flags, flags])
    return jnp.where(paired == 1, (slots_all + half) % N_EXPERT, slots_all).astype(jnp.int32)


def shard_levels(stream_key, extent, cuts, least, top_value):
    gain = 1.0
    for dim, shards_of in cuts:
        steps = jax.random.uniform(jax.random.fold_in(jax.random.fold_in(stream_key, 6), dim), (shards_of,), jnp.float32, least / len(cuts), top_value / len(cuts))
        gain = gain * jnp.repeat(jnp.exp(steps), extent[dim] // shards_of).reshape((-1,) + (1,) * (len(extent) - 1 - dim))
    return gain


def normal_values(own_key, shape, spread, limit, cuts=(), held_as=jnp.bfloat16):
    array = jax.random.normal(own_key, shape, jnp.float32) * spread
    if len(cuts) > 0:
        array = shard_levels(own_key, shape, cuts, -0.22, 0.18) * array
    return jnp.clip(array, min=-limit, max=limit).astype(held_as)


def setup_inputs(seed: int = 0, part: int = 0) -> dict:
    key_of = jax.random.split(jax.random.key(seed), 7)
    own_keys = jax.random.split(jax.random.fold_in(key_of[6], part), 7)
    return {
        "tokens": normal_values(own_keys[0], (TOKENS, D), 1.0, 6.0, ((0, 16),)),
        "affinity": jnp.clip(jnp.exp(math.log(1.0) - 2.9957323 * jax.random.uniform(own_keys[1], (TOKENS, TOP), jnp.float32) ** shard_levels(own_keys[1], (TOKENS, TOP), ((0, 16),), -0.2, 0.2)), 0.05, 1.0),
        "expert_ids": draw_expert_ids(jax.random.fold_in(jax.random.fold_in(key_of[6], part), 71), part),
        "swap_partner": draw_swap_partner(jax.random.fold_in(jax.random.fold_in(key_of[6], part), 71), part),
        "gate_up": normal_values(key_of[4], (N_EXPERT, 2, D, HID), 1.0, 6.0, ((0, 4), (3, 4))),
        "down_proj": normal_values(key_of[5], (N_EXPERT, HID, D), 1.0, 6.0, ((0, 4), (1, 4))),
    }


scale_mix = 2.5


def reference(tokens, affinity, expert_ids, swap_partner, gate_up, down_proj):
    n_blocks = TOKENS // TOK_DEV
    unit_width = HID // N_DP
    slot_total = n_blocks * CAP
    new_gate_up = jnp.take(gate_up, swap_partner, axis=0)
    new_down = jnp.take(down_proj, swap_partner, axis=0)
    mixing = scale_mix * affinity / jnp.sum(affinity, axis=1, keepdims=True)
    chosen = (expert_ids[:, :, None] == jnp.arange(N_EXPERT, dtype=jnp.int32)[None, None, :]).astype(jnp.int32)
    per_token = jnp.sum(chosen, axis=1)
    mix_table = jnp.sum(jnp.where(chosen > 0, mixing[:, :, None], jnp.zeros_like(mixing)[:, :, None]), axis=1)
    blocked = per_token.reshape(n_blocks, TOK_DEV, N_EXPERT)
    rank_table = (jnp.cumsum(blocked, axis=1) - blocked).reshape(TOKENS, N_EXPERT)
    token_index = jnp.arange(TOKENS, dtype=jnp.int32)
    slot_table = (token_index // TOK_DEV)[:, None] * CAP + rank_table
    slot_table = jnp.where(per_token > 0, slot_table, slot_total).astype(jnp.int32)
    expert_grid = jnp.broadcast_to(jnp.arange(N_EXPERT, dtype=jnp.int32)[None, :], (TOKENS, N_EXPERT))
    token_grid = jnp.broadcast_to(token_index[:, None], (TOKENS, N_EXPERT))
    row_table = jnp.full((N_EXPERT, slot_total + 1), TOKENS, jnp.int32)
    row_table = row_table.at[expert_grid, slot_table].set(token_grid)[:, :slot_total]
    padded = jnp.concatenate([tokens, jnp.zeros((1, D), tokens.dtype)], axis=0)
    clamped = jnp.minimum(slot_table, slot_total - 1).astype(jnp.int32)

    def add_expert(expert_index, running):
        row_block = jnp.take(padded, row_table[expert_index], axis=0)
        weights_in = gate_up[expert_index]
        gate_value = jnp.dot(row_block, weights_in[0], preferred_element_type=jnp.float32) * (D ** -0.5)
        up_value = jnp.dot(row_block, weights_in[1], preferred_element_type=jnp.float32) * (D ** -0.5)
        hidden = (jax.nn.silu(gate_value) * up_value).astype(jnp.bfloat16)
        pieces = jnp.einsum(
            "sjh,jhd->sjd",
            hidden.reshape(slot_total, N_DP, unit_width).astype(jnp.float32),
            down_proj[expert_index].reshape(N_DP, unit_width, D).astype(jnp.float32),
        ) * (HID ** -0.5)
        pieces = lax.optimization_barrier(pieces.astype(jnp.bfloat16)).astype(jnp.float32)
        expert_out = jnp.sum(pieces, axis=1)
        picked = jnp.take(expert_out, clamped[:, expert_index], axis=0)
        return running + mix_table[:, expert_index][:, None] * picked

    running = lax.fori_loop(0, N_EXPERT, add_expert, jnp.zeros((TOKENS, D), jnp.float32))
    return running.astype(jnp.bfloat16), new_gate_up, new_down
```

```python
import functools

import jax
import jax.numpy as jnp
from jax import lax
from jax.experimental import pallas as pl
from jax.experimental.pallas import tpu as pltpu
from jax.sharding import PartitionSpec as P

CAP = 2
TILE_ROWS = 16
SEGS = TILE_ROWS // CAP
WINDOW = 4
GU_PIECES = 16
scale_mix = 2.5
MESH = pl.DeviceIdType.MESH


def kernel(
    n_expert,
    n_dp,
    ids_ref,
    aff_ref,
    tok_ref,
    gu_ref,
    dn_ref,
    sgu_ref,
    sdn_ref,
    moe_ref,
    send_buf,
    arrived,
    out_buf,
    returned,
    acc,
    down_acc,
    sums,
    gu_vmem,
    dn_vmem,
    load_sem,
    tok_send,
    tok_recv,
    ret_send,
    ret_recv,
    y_send,
    y_recv,
    x_send,
    x_recv,
):
    g = lax.axis_index("group")
    e = lax.axis_index("expert")
    d = lax.axis_index("dp")
    peers = n_expert * n_dp
    me = e * n_dp + d
    half = n_expert // 2
    partner = lax.rem(e + half, n_expert)
    other = 1 - g
    tokens, width = tok_ref.shape
    top = ids_ref.shape[0]
    seg = width * CAP // TILE_ROWS
    hid = gu_ref.shape[3]

    loads = [
        pltpu.make_async_copy(gu_ref.at[0], gu_vmem, load_sem.at[0]),
        pltpu.make_async_copy(dn_ref.at[0], dn_vmem, load_sem.at[1]),
    ]
    for load in loads:
        load.start()

    barrier = pltpu.get_barrier_semaphore()

    def greet(i, carry):
        p = lax.rem(me + i, peers)
        pl.semaphore_signal(
            barrier, inc=1, device_id=(g, p // n_dp, lax.rem(p, n_dp)), device_id_type=MESH
        )
        return carry

    lax.fori_loop(1, peers, greet, 0)
    pl.semaphore_signal(barrier, inc=1, device_id=(other, e, d), device_id_type=MESH)

    table_rows = n_expert * TILE_ROWS
    row = lax.broadcasted_iota(jnp.int32, (table_rows, tokens), 0)
    expert_of = row // TILE_ROWS
    place_of = lax.rem(row // SEGS, CAP)
    ids = ids_ref[...]
    aff = aff_ref[...]
    mixing = scale_mix * aff / jnp.sum(aff, axis=0, keepdims=True)
    picked = jnp.zeros((table_rows, tokens), jnp.float32)
    mixed = jnp.zeros((table_rows, tokens), jnp.float32)
    for i in range(top):
        hit = ids[i : i + 1, :] == expert_of
        picked = picked + jnp.where(hit, 1.0, 0.0)
        mixed = mixed + jnp.where(hit, mixing[i : i + 1, :], 0.0)
    earlier = lax.broadcasted_iota(jnp.int32, (tokens, tokens), 0) < lax.broadcasted_iota(
        jnp.int32, (tokens, tokens), 1
    )
    rank = jnp.dot(
        picked.astype(jnp.bfloat16),
        jnp.where(earlier, 1.0, 0.0).astype(jnp.bfloat16),
        preferred_element_type=jnp.float32,
    )
    chosen = (picked > 0.5) & (rank.astype(jnp.int32) == place_of)
    dispatch = jnp.where(chosen, 1.0, 0.0).astype(jnp.bfloat16)
    combine = jnp.where(chosen, mixed, 0.0)
    piece_row = lax.rem(lax.broadcasted_iota(jnp.int32, (table_rows, seg), 0), SEGS)
    outgoing = jnp.zeros((table_rows, seg), jnp.float32)
    for s in range(SEGS):
        part = jnp.dot(
            dispatch, tok_ref[:, s * seg : (s + 1) * seg], preferred_element_type=jnp.float32
        )
        outgoing = jnp.where(piece_row == s, part, outgoing)
    send_buf[...] = outgoing.astype(jnp.bfloat16).reshape(send_buf.shape)
    arrived[me] = send_buf[e]

    pl.semaphore_wait(barrier, peers)

    def token_copy(p, slot_there):
        return pltpu.make_async_remote_copy(
            src_ref=send_buf.at[p // n_dp],
            dst_ref=arrived.at[slot_there],
            send_sem=tok_send.at[p],
            recv_sem=tok_recv.at[slot_there],
            device_id=(g, p // n_dp, lax.rem(p, n_dp)),
            device_id_type=MESH,
        )

    def return_copy(p, slot_there):
        return pltpu.make_async_remote_copy(
            src_ref=out_buf.at[p],
            dst_ref=returned.at[slot_there],
            send_sem=ret_send.at[p],
            recv_sem=ret_recv.at[slot_there],
            device_id=(g, p // n_dp, lax.rem(p, n_dp)),
            device_id_type=MESH,
        )

    def each_peer(act):
        def step(i, carry):
            act(lax.rem(me + i, peers))
            return carry

        lax.fori_loop(1, peers, step, 0)

    each_peer(lambda p: token_copy(p, me).start())

    gu_rows = width // GU_PIECES
    dn_half = hid // 2
    dn_pieces = dn_half // TILE_ROWS
    pieces = GU_PIECES + dn_pieces

    def place(own, swapped, k, which):
        if k < GU_PIECES:
            rows = pl.ds(k * gu_rows, gu_rows)
            return gu_ref.at[0, which, rows] if own else sgu_ref.at[0, which, rows]
        start = pl.multiple_of(which * dn_half + (k - GU_PIECES) * TILE_ROWS, TILE_ROWS)
        rows = pl.ds(start, TILE_ROWS)
        return dn_ref.at[0, rows] if own else sdn_ref.at[0, rows]

    def to_partner(k):
        return pltpu.make_async_remote_copy(
            src_ref=place(True, False, k, g),
            dst_ref=place(False, True, k, g),
            send_sem=y_send.at[k],
            recv_sem=y_recv.at[k],
            device_id=(g, partner, d),
            device_id_type=MESH,
        )

    def to_group(k, which):
        return pltpu.make_async_remote_copy(
            src_ref=place(False, True, k, which),
            dst_ref=place(False, True, k, which),
            send_sem=x_send.at[k],
            recv_sem=x_recv.at[k],
            device_id=(other, e, d),
            device_id_type=MESH,
        )

    for k in range(min(WINDOW, pieces)):
        to_partner(k).start()

    def forward(k):
        copy = to_partner(k)
        copy.wait_recv()
        to_group(k, g).start()
        copy.wait_send()
        if k + WINDOW < pieces:
            to_partner(k + WINDOW).start()

    for load in loads:
        load.wait()
    each_peer(lambda p: token_copy(p, p).wait_recv())

    block = min(256, peers * TILE_ROWS)
    groups = block // TILE_ROWS

    def expert_block(b, carry):
        start = pl.multiple_of(b * groups, groups)
        rows_in = arrived[pl.ds(start, groups)].reshape(block, seg)
        piece = lax.rem(lax.broadcasted_iota(jnp.int32, (block, hid), 0), SEGS)
        for half_of in range(2):
            total = jnp.zeros((block, hid), jnp.float32)
            for s in range(SEGS):
                part = jnp.dot(
                    rows_in,
                    gu_vmem[half_of, s * seg : (s + 1) * seg, :],
                    preferred_element_type=jnp.float32,
                )
                total = total + jnp.where(piece == s, part, 0.0)
            acc[half_of] = jnp.sum(total.reshape(block // SEGS, SEGS, hid), axis=1)
        gate = acc[0] * width ** (-0.5)
        up = acc[1] * width ** (-0.5)
        hidden = gate / (1.0 + jnp.exp(-gate)) * up
        spread = jnp.broadcast_to(hidden[:, None, :], (block // SEGS, SEGS, hid))
        spread = spread.reshape(block, hid).astype(jnp.bfloat16)
        out_piece = lax.rem(lax.broadcasted_iota(jnp.int32, (block, seg), 0), SEGS)
        for s in range(SEGS):
            part = jnp.dot(
                spread,
                dn_vmem[:, s * seg : (s + 1) * seg],
                preferred_element_type=jnp.float32,
            )
            down_acc[...] = part if s == 0 else jnp.where(out_piece == s, part, down_acc[...])
        scaled = down_acc[...] * (hid * n_dp) ** (-0.5)
        out_buf[pl.ds(start, groups)] = scaled.astype(jnp.bfloat16).reshape(groups, TILE_ROWS, seg)
        return carry

    lax.fori_loop(0, peers * TILE_ROWS // block, expert_block, 0)
    returned[me] = out_buf[me]
    each_peer(lambda p: return_copy(p, me).start())

    late = pieces // 2
    for k in range(late):
        forward(k)

    each_peer(lambda p: return_copy(p, p).wait_recv())
    for j in range(n_expert):
        total = returned[j * n_dp].astype(jnp.float32)
        for i in range(1, n_dp):
            total = total + returned[j * n_dp + i].astype(jnp.float32)
        sums[j * TILE_ROWS : (j + 1) * TILE_ROWS, :] = total
    weights = combine.T
    column = lax.rem(lax.broadcasted_iota(jnp.int32, (tokens, table_rows), 1), SEGS)
    for s in range(SEGS):
        moe = jnp.dot(
            jnp.where(column == s, weights, 0.0),
            sums[...],
            precision=lax.Precision.HIGHEST,
            preferred_element_type=jnp.float32,
        )
        moe_ref[:, s * seg : (s + 1) * seg] = moe.astype(jnp.bfloat16)

    for k in range(late, pieces):
        forward(k)

    each_peer(lambda p: token_copy(p, p).wait_send())
    each_peer(lambda p: return_copy(p, p).wait_send())
    for k in range(pieces):
        to_group(k, g).wait_send()
        to_group(k, other).wait_recv()


def exchange(n_expert, n_dp, expert_ids, affinity, tokens, gate_up, down_proj):
    rows, width = tokens.shape
    hid = gate_up.shape[3]
    peers = n_expert * n_dp
    seg = width * CAP // TILE_ROWS
    block = min(256, peers * TILE_ROWS)
    pieces = GU_PIECES + hid // 2 // TILE_ROWS
    vmem = pl.BlockSpec(memory_space=pltpu.VMEM)
    hbm = pl.BlockSpec(memory_space=pl.ANY)
    return pl.pallas_call(
        functools.partial(kernel, n_expert, n_dp),
        out_shape=(
            jax.ShapeDtypeStruct(gate_up.shape, jnp.bfloat16),
            jax.ShapeDtypeStruct(down_proj.shape, jnp.bfloat16),
            jax.ShapeDtypeStruct(tokens.shape, jnp.bfloat16),
        ),
        in_specs=[vmem, vmem, vmem, hbm, hbm],
        out_specs=(hbm, hbm, vmem),
        scratch_shapes=[
            pltpu.VMEM((n_expert, TILE_ROWS, seg), jnp.bfloat16),
            pltpu.VMEM((peers, TILE_ROWS, seg), jnp.bfloat16),
            pltpu.VMEM((peers, TILE_ROWS, seg), jnp.bfloat16),
            pltpu.VMEM((peers, TILE_ROWS, seg), jnp.bfloat16),
            pltpu.VMEM((2, block // SEGS, hid), jnp.float32),
            pltpu.VMEM((block, seg), jnp.float32),
            pltpu.VMEM((n_expert * TILE_ROWS, seg), jnp.float32),
            pltpu.VMEM(gate_up.shape[1:], jnp.bfloat16),
            pltpu.VMEM(down_proj.shape[1:], jnp.bfloat16),
            pltpu.SemaphoreType.DMA((2,)),
            pltpu.SemaphoreType.DMA((peers,)),
            pltpu.SemaphoreType.DMA((peers,)),
            pltpu.SemaphoreType.DMA((peers,)),
            pltpu.SemaphoreType.DMA((peers,)),
            pltpu.SemaphoreType.DMA((pieces,)),
            pltpu.SemaphoreType.DMA((pieces,)),
            pltpu.SemaphoreType.DMA((pieces,)),
            pltpu.SemaphoreType.DMA((pieces,)),
        ],
        compiler_params=pltpu.CompilerParams(
            collective_id=0, has_side_effects=True, vmem_limit_bytes=40 * 2**20
        ),
        cost_estimate=pl.CostEstimate(
            flops=2 * peers * TILE_ROWS * 3 * hid * width,
            bytes_accessed=8 * hid * width * 3,
            transcendentals=peers * CAP * hid,
        ),
    )(expert_ids.T, affinity.T, tokens, gate_up, down_proj)


def per_device(n_expert, n_dp, tokens, affinity, expert_ids, swap_partner, gate_up, down_proj):
    swapped_gate_up, swapped_down, moe_out = exchange(
        n_expert, n_dp, expert_ids, affinity, tokens, gate_up, down_proj
    )
    myself = lax.axis_index("expert")
    changed = swap_partner[myself] != myself
    new_gate_up = jnp.where(changed, swapped_gate_up, gate_up)
    new_down = jnp.where(changed, swapped_down, down_proj)
    return (moe_out, new_gate_up, new_down)


def solution(mesh):
    placed = (
        P(("group", "expert", "dp"), None),
        P(("group", "expert", "dp"), None),
        P(("group", "expert", "dp"), None),
        P("group"),
        P("expert", None, None, "dp"),
        P("expert", "dp", None),
    )
    return jax.shard_map(
        functools.partial(per_device, mesh.shape["expert"], mesh.shape["dp"]),
        mesh=mesh,
        in_specs=placed,
        out_specs=(
            P(("group", "expert", "dp"), None),
            P(("group", "expert"), None, None, "dp"),
            P(("group", "expert"), "dp", None),
        ),
        check_vma=False,
    )
```

```python
import functools

import jax
import jax.numpy as jnp
from jax import lax
from jax.experimental import pallas as pl
from jax.experimental.pallas import tpu as pltpu
from jax.sharding import PartitionSpec as P

CAP = 2
TILE_ROWS = 16
SEGS = TILE_ROWS // CAP
WINDOW = 5
GU_PIECES = 16
LAG = 3
scale_mix = 2.5
MESH = pl.DeviceIdType.MESH


def kernel(
    n_expert,
    n_dp,
    ids_hbm,
    aff_hbm,
    swap_hbm,
    tok_hbm,
    gu_ref,
    dn_ref,
    sgu_ref,
    sdn_ref,
    moe_ref,
    ids_ref,
    aff_ref,
    swap_ref,
    tok_ref,
    send_buf,
    arrived,
    out_buf,
    returned,
    acc,
    down_acc,
    sums,
    gu_vmem,
    dn_vmem,
    load_sem,
    tok_send,
    tok_recv,
    ret_send,
    ret_recv,
    y_send,
    y_recv,
    x_send,
    x_recv,
):
    g = lax.axis_index("group")
    e = lax.axis_index("expert")
    d = lax.axis_index("dp")
    peers = n_expert * n_dp
    me = e * n_dp + d
    half = n_expert // 2
    partner = lax.rem(e + half, n_expert)
    other = 1 - g
    tokens, width = tok_ref.shape
    top = ids_ref.shape[0]
    seg = width * CAP // TILE_ROWS
    hid = gu_ref.shape[3]

    loads = [
        pltpu.make_async_copy(gu_ref.at[0], gu_vmem, load_sem.at[0]),
        pltpu.make_async_copy(dn_ref.at[0], dn_vmem, load_sem.at[1]),
    ]
    small = [
        pltpu.make_async_copy(ids_hbm, ids_ref, load_sem.at[2]),
        pltpu.make_async_copy(aff_hbm, aff_ref, load_sem.at[3]),
        pltpu.make_async_copy(swap_hbm, swap_ref, load_sem.at[4]),
        pltpu.make_async_copy(tok_hbm, tok_ref, load_sem.at[5]),
    ]
    for load in small:
        load.start()

    barrier = pltpu.get_barrier_semaphore()

    def greet(i, carry):
        p = lax.rem(me + i, peers)
        pl.semaphore_signal(
            barrier, inc=1, device_id=(g, p // n_dp, lax.rem(p, n_dp)), device_id_type=MESH
        )
        return carry

    lax.fori_loop(1, peers, greet, 0)
    pl.semaphore_signal(barrier, inc=1, device_id=(other, e, d), device_id_type=MESH)

    pl.semaphore_wait(barrier, peers)

    def token_copy(p, slot_there):
        return pltpu.make_async_remote_copy(
            src_ref=send_buf.at[p // n_dp],
            dst_ref=arrived.at[slot_there],
            send_sem=tok_send.at[p],
            recv_sem=tok_recv.at[slot_there],
            device_id=(g, p // n_dp, lax.rem(p, n_dp)),
            device_id_type=MESH,
        )

    def return_copy(p, slot_there):
        return pltpu.make_async_remote_copy(
            src_ref=out_buf.at[p],
            dst_ref=returned.at[slot_there],
            send_sem=ret_send.at[p],
            recv_sem=ret_recv.at[slot_there],
            device_id=(g, p // n_dp, lax.rem(p, n_dp)),
            device_id_type=MESH,
        )

    def each_peer(act):
        def step(i, carry):
            act(lax.rem(me + i, peers))
            return carry

        lax.fori_loop(1, peers, step, 0)

    gu_rows = width // GU_PIECES
    dn_half = hid // 2
    dn_pieces = dn_half // TILE_ROWS
    pieces = GU_PIECES + dn_pieces
    early, late = pieces // 4, pieces * 2 // 3

    def place(own, swapped, k, which):
        if k < GU_PIECES:
            rows = pl.ds(k * gu_rows, gu_rows)
            return gu_ref.at[0, which, rows] if own else sgu_ref.at[0, which, rows]
        start = pl.multiple_of(which * dn_half + (k - GU_PIECES) * TILE_ROWS, TILE_ROWS)
        rows = pl.ds(start, TILE_ROWS)
        return dn_ref.at[0, rows] if own else sdn_ref.at[0, rows]

    def to_partner(k):
        return pltpu.make_async_remote_copy(
            src_ref=place(True, False, k, g),
            dst_ref=place(False, True, k, g),
            send_sem=y_send.at[k],
            recv_sem=y_recv.at[k],
            device_id=(g, partner, d),
            device_id_type=MESH,
        )

    def to_group(k, which):
        return pltpu.make_async_remote_copy(
            src_ref=place(False, True, k, which),
            dst_ref=place(False, True, k, which),
            send_sem=x_send.at[k],
            recv_sem=x_recv.at[k],
            device_id=(other, e, d),
            device_id_type=MESH,
        )

    for k in range(min(WINDOW, pieces)):
        to_partner(k).start()
    for load in loads:
        load.start()
    for load in small:
        load.wait()

    table_rows = n_expert * TILE_ROWS
    row = lax.broadcasted_iota(jnp.int32, (table_rows, tokens), 0)
    expert_of = row // TILE_ROWS
    place_of = lax.rem(row // SEGS, CAP)
    ids = ids_ref[...]
    aff = aff_ref[...]
    mixing = scale_mix * aff / jnp.sum(aff, axis=0, keepdims=True)
    picked = jnp.zeros((table_rows, tokens), jnp.float32)
    mixed = jnp.zeros((table_rows, tokens), jnp.float32)
    for i in range(top):
        hit = ids[i : i + 1, :] == expert_of
        picked = picked + jnp.where(hit, 1.0, 0.0)
        mixed = mixed + jnp.where(hit, mixing[i : i + 1, :], 0.0)
    earlier = lax.broadcasted_iota(jnp.int32, (tokens, tokens), 0) < lax.broadcasted_iota(
        jnp.int32, (tokens, tokens), 1
    )
    rank = jnp.dot(
        picked.astype(jnp.bfloat16),
        jnp.where(earlier, 1.0, 0.0).astype(jnp.bfloat16),
        preferred_element_type=jnp.float32,
    )
    chosen = (picked > 0.5) & (rank.astype(jnp.int32) == place_of)
    dispatch = jnp.where(chosen, 1.0, 0.0).astype(jnp.bfloat16)
    combine = jnp.where(chosen, mixed, 0.0)
    piece_row = lax.rem(lax.broadcasted_iota(jnp.int32, (table_rows, seg), 0), SEGS)
    outgoing = jnp.zeros((table_rows, seg), jnp.float32)
    for s in range(SEGS):
        part = jnp.dot(
            dispatch, tok_ref[:, s * seg : (s + 1) * seg], preferred_element_type=jnp.float32
        )
        outgoing = jnp.where(piece_row == s, part, outgoing)
    send_buf[...] = outgoing.astype(jnp.bfloat16).reshape(send_buf.shape)
    arrived[me] = send_buf[e]

    each_peer(lambda p: token_copy(p, me).start())
    changed = swap_ref[e] != e

    def forward(k):
        copy = to_partner(k)
        copy.wait_recv()
        to_group(k, g).start()
        copy.wait_send()
        if k + WINDOW < pieces:
            to_partner(k + WINDOW).start()

    def choose(k, which):
        shape = (gu_rows, hid) if k < GU_PIECES else (TILE_ROWS, width)
        took = jnp.broadcast_to(jnp.where(changed, 1, 0), shape) == 1
        if k < GU_PIECES:
            rows = pl.ds(k * gu_rows, gu_rows)
            new = sgu_ref[0, which, rows].astype(jnp.float32)
            old = gu_vmem[which, rows].astype(jnp.float32)
            sgu_ref[0, which, rows] = jnp.where(took, new, old).astype(jnp.bfloat16)
        else:
            start = which * dn_half + (k - GU_PIECES) * TILE_ROWS
            rows = pl.ds(pl.multiple_of(start, TILE_ROWS), TILE_ROWS)
            new = sdn_ref[0, rows].astype(jnp.float32)
            old = dn_vmem[rows].astype(jnp.float32)
            sdn_ref[0, rows] = jnp.where(took, new, old).astype(jnp.bfloat16)

    def settle(k):
        to_group(k, g).wait_send()
        choose(k, g)
        to_group(k, other).wait_recv()
        choose(k, other)

    for k in range(early):
        forward(k)
    for load in loads:
        load.wait()
    each_peer(lambda p: token_copy(p, p).wait_recv())

    block = min(256, peers * TILE_ROWS)
    groups = block // TILE_ROWS

    def expert_block(b, carry):
        start = pl.multiple_of(b * groups, groups)
        rows_in = arrived[pl.ds(start, groups)].reshape(block, seg)
        piece = lax.rem(lax.broadcasted_iota(jnp.int32, (block, hid), 0), SEGS)
        for half_of in range(2):
            total = jnp.zeros((block, hid), jnp.float32)
            for s in range(SEGS):
                part = jnp.dot(
                    rows_in,
                    gu_vmem[half_of, s * seg : (s + 1) * seg, :],
                    preferred_element_type=jnp.float32,
                )
                total = total + jnp.where(piece == s, part, 0.0)
            acc[half_of] = jnp.sum(total.reshape(block // SEGS, SEGS, hid), axis=1)
        gate = acc[0] * width ** (-0.5)
        up = acc[1] * width ** (-0.5)
        hidden = gate / (1.0 + jnp.exp(-gate)) * up
        spread = jnp.broadcast_to(hidden[:, None, :], (block // SEGS, SEGS, hid))
        spread = spread.reshape(block, hid).astype(jnp.bfloat16)
        out_piece = lax.rem(lax.broadcasted_iota(jnp.int32, (block, seg), 0), SEGS)
        for s in range(SEGS):
            part = jnp.dot(
                spread,
                dn_vmem[:, s * seg : (s + 1) * seg],
                preferred_element_type=jnp.float32,
            )
            down_acc[...] = part if s == 0 else jnp.where(out_piece == s, part, down_acc[...])
        scaled = down_acc[...] * (hid * n_dp) ** (-0.5)
        out_buf[pl.ds(start, groups)] = scaled.astype(jnp.bfloat16).reshape(groups, TILE_ROWS, seg)
        return carry

    lax.fori_loop(0, peers * TILE_ROWS // block, expert_block, 0)
    returned[me] = out_buf[me]
    each_peer(lambda p: return_copy(p, me).start())

    for k in range(early - LAG):
        settle(k)
    for k in range(early, late):
        forward(k)
        settle(k - LAG)

    each_peer(lambda p: return_copy(p, p).wait_recv())
    for j in range(n_expert):
        total = returned[j * n_dp].astype(jnp.float32)
        for i in range(1, n_dp):
            total = total + returned[j * n_dp + i].astype(jnp.float32)
        sums[j * TILE_ROWS : (j + 1) * TILE_ROWS, :] = total
    weights = combine.T
    column = lax.rem(lax.broadcasted_iota(jnp.int32, (tokens, table_rows), 1), SEGS)
    for s in range(SEGS):
        moe = jnp.dot(
            jnp.where(column == s, weights, 0.0),
            sums[...],
            precision=lax.Precision.HIGHEST,
            preferred_element_type=jnp.float32,
        )
        moe_ref[:, s * seg : (s + 1) * seg] = moe.astype(jnp.bfloat16)

    for k in range(late, pieces):
        forward(k)
        settle(k - LAG)

    each_peer(lambda p: token_copy(p, p).wait_send())
    each_peer(lambda p: return_copy(p, p).wait_send())
    for k in range(pieces - LAG, pieces):
        settle(k)


def exchange(n_expert, n_dp, expert_ids, affinity, swap_partner, tokens, gate_up, down_proj):
    rows, width = tokens.shape
    hid = gate_up.shape[3]
    peers = n_expert * n_dp
    seg = width * CAP // TILE_ROWS
    block = min(256, peers * TILE_ROWS)
    pieces = GU_PIECES + hid // 2 // TILE_ROWS
    vmem = pl.BlockSpec(memory_space=pltpu.VMEM)
    hbm = pl.BlockSpec(memory_space=pltpu.HBM)
    return pl.pallas_call(
        functools.partial(kernel, n_expert, n_dp),
        out_shape=(
            pltpu.VMEM(gate_up.shape, jnp.bfloat16),
            pltpu.VMEM(down_proj.shape, jnp.bfloat16),
            pltpu.VMEM(tokens.shape, jnp.bfloat16),
        ),
        in_specs=[hbm] * 6,
        out_specs=(vmem, vmem, vmem),
        scratch_shapes=[
            pltpu.VMEM(expert_ids.shape[::-1], jnp.int32),
            pltpu.VMEM(affinity.shape[::-1], jnp.float32),
            pltpu.SMEM(swap_partner.shape, jnp.int32),
            pltpu.VMEM(tokens.shape, jnp.bfloat16),
            pltpu.VMEM((n_expert, TILE_ROWS, seg), jnp.bfloat16),
            pltpu.VMEM((peers, TILE_ROWS, seg), jnp.bfloat16),
            pltpu.VMEM((peers, TILE_ROWS, seg), jnp.bfloat16),
            pltpu.VMEM((peers, TILE_ROWS, seg), jnp.bfloat16),
            pltpu.VMEM((2, block // SEGS, hid), jnp.float32),
            pltpu.VMEM((block, seg), jnp.float32),
            pltpu.VMEM((n_expert * TILE_ROWS, seg), jnp.float32),
            pltpu.VMEM(gate_up.shape[1:], jnp.bfloat16),
            pltpu.VMEM(down_proj.shape[1:], jnp.bfloat16),
            pltpu.SemaphoreType.DMA((6,)),
            pltpu.SemaphoreType.DMA((peers,)),
            pltpu.SemaphoreType.DMA((peers,)),
            pltpu.SemaphoreType.DMA((peers,)),
            pltpu.SemaphoreType.DMA((peers,)),
            pltpu.SemaphoreType.DMA((pieces,)),
            pltpu.SemaphoreType.DMA((pieces,)),
            pltpu.SemaphoreType.DMA((pieces,)),
            pltpu.SemaphoreType.DMA((pieces,)),
        ],
        compiler_params=pltpu.CompilerParams(
            collective_id=0, has_side_effects=True, vmem_limit_bytes=52 * 2**20
        ),
        cost_estimate=pl.CostEstimate(
            flops=2 * peers * TILE_ROWS * 3 * hid * width,
            bytes_accessed=8 * hid * width * 3,
            transcendentals=peers * CAP * hid,
        ),
    )(expert_ids.T, affinity.T, swap_partner, tokens, gate_up, down_proj)


def per_device(n_expert, n_dp, tokens, affinity, expert_ids, swap_partner, gate_up, down_proj):
    new_gate_up, new_down, moe_out = exchange(
        n_expert, n_dp, expert_ids, affinity, swap_partner, tokens, gate_up, down_proj
    )
    return (moe_out, new_gate_up, new_down)


def solution(mesh):
    placed = (
        P(("group", "expert", "dp"), None),
        P(("group", "expert", "dp"), None),
        P(("group", "expert", "dp"), None),
        P("group"),
        P("expert", None, None, "dp"),
        P("expert", "dp", None),
    )
    return jax.shard_map(
        functools.partial(per_device, mesh.shape["expert"], mesh.shape["dp"]),
        mesh=mesh,
        in_specs=placed,
        out_specs=(
            P(("group", "expert", "dp"), None),
            P(("group", "expert"), None, None, "dp"),
            P(("group", "expert"), "dp", None),
        ),
        check_vma=False,
    )
```

```python
import functools

import jax
import jax.numpy as jnp
from jax import lax
from jax.experimental import pallas as pl
from jax.experimental.pallas import tpu as pltpu
from jax.sharding import PartitionSpec as P

CAP = 2
TILE_ROWS = 16
SEGS = TILE_ROWS // CAP
WINDOW = 5
GU_PIECES = 32
LAG = 3
scale_mix = 2.5
MESH = pl.DeviceIdType.MESH


def kernel(
    n_expert,
    n_dp,
    ids_hbm,
    aff_hbm,
    swap_hbm,
    tok_hbm,
    gu_ref,
    dn_ref,
    sgu_ref,
    sdn_ref,
    moe_ref,
    ids_ref,
    aff_ref,
    swap_ref,
    tok_ref,
    send_buf,
    arrived,
    out_buf,
    returned,
    acc,
    down_acc,
    sums,
    gu_vmem,
    dn_vmem,
    load_sem,
    tok_send,
    tok_recv,
    ret_send,
    ret_recv,
    y_send,
    y_recv,
    x_send,
    x_recv,
):
    g = lax.axis_index("group")
    e = lax.axis_index("expert")
    d = lax.axis_index("dp")
    peers = n_expert * n_dp
    me = e * n_dp + d
    half = n_expert // 2
    partner = lax.rem(e + half, n_expert)
    other = 1 - g
    tokens, width = tok_ref.shape
    top = ids_ref.shape[0]
    seg = width * CAP // TILE_ROWS
    hid = gu_ref.shape[3]

    loads = [
        pltpu.make_async_copy(gu_ref.at[0], gu_vmem, load_sem.at[0]),
        pltpu.make_async_copy(dn_ref.at[0], dn_vmem, load_sem.at[1]),
    ]
    small = [
        pltpu.make_async_copy(ids_hbm, ids_ref, load_sem.at[2]),
        pltpu.make_async_copy(aff_hbm, aff_ref, load_sem.at[3]),
        pltpu.make_async_copy(swap_hbm, swap_ref, load_sem.at[4]),
        pltpu.make_async_copy(tok_hbm, tok_ref, load_sem.at[5]),
    ]
    for load in small:
        load.start()

    barrier = pltpu.get_barrier_semaphore()

    def greet(i, carry):
        p = lax.rem(me + i, peers)
        pl.semaphore_signal(
            barrier, inc=1, device_id=(g, p // n_dp, lax.rem(p, n_dp)), device_id_type=MESH
        )
        return carry

    lax.fori_loop(1, peers, greet, 0)
    pl.semaphore_signal(barrier, inc=1, device_id=(other, e, d), device_id_type=MESH)

    pl.semaphore_wait(barrier, peers)

    def token_copy(p, slot_there):
        return pltpu.make_async_remote_copy(
            src_ref=send_buf.at[p // n_dp],
            dst_ref=arrived.at[slot_there],
            send_sem=tok_send.at[p],
            recv_sem=tok_recv.at[slot_there],
            device_id=(g, p // n_dp, lax.rem(p, n_dp)),
            device_id_type=MESH,
        )

    def return_copy(p, slot_there):
        return pltpu.make_async_remote_copy(
            src_ref=out_buf.at[p],
            dst_ref=returned.at[slot_there],
            send_sem=ret_send.at[p],
            recv_sem=ret_recv.at[slot_there],
            device_id=(g, p // n_dp, lax.rem(p, n_dp)),
            device_id_type=MESH,
        )

    def each_peer(act):
        def step(i, carry):
            act(lax.rem(me + i, peers))
            return carry

        lax.fori_loop(1, peers, step, 0)

    gu_rows = width // GU_PIECES
    dn_half = hid // 2
    dn_pieces = dn_half // TILE_ROWS
    pieces = GU_PIECES + dn_pieces
    early, late = pieces // 4, pieces * 2 // 3

    def place(own, swapped, k, which):
        k = pieces - 1 - k
        if k < GU_PIECES:
            rows = pl.ds(k * gu_rows, gu_rows)
            return gu_ref.at[0, which, rows] if own else sgu_ref.at[0, which, rows]
        start = pl.multiple_of(which * dn_half + (k - GU_PIECES) * TILE_ROWS, TILE_ROWS)
        rows = pl.ds(start, TILE_ROWS)
        return dn_ref.at[0, rows] if own else sdn_ref.at[0, rows]

    def to_partner(k):
        return pltpu.make_async_remote_copy(
            src_ref=place(True, False, k, g),
            dst_ref=place(False, True, k, g),
            send_sem=y_send.at[k],
            recv_sem=y_recv.at[k],
            device_id=(g, partner, d),
            device_id_type=MESH,
        )

    def to_group(k, which):
        return pltpu.make_async_remote_copy(
            src_ref=place(False, True, k, which),
            dst_ref=place(False, True, k, which),
            send_sem=x_send.at[k],
            recv_sem=x_recv.at[k],
            device_id=(other, e, d),
            device_id_type=MESH,
        )

    for k in range(min(WINDOW, pieces)):
        to_partner(k).start()
    for load in loads:
        load.start()
    for load in small:
        load.wait()

    table_rows = n_expert * TILE_ROWS
    row = lax.broadcasted_iota(jnp.int32, (table_rows, tokens), 0)
    expert_of = row // TILE_ROWS
    place_of = lax.rem(row // SEGS, CAP)
    ids = ids_ref[...]
    aff = aff_ref[...]
    mixing = scale_mix * aff / jnp.sum(aff, axis=0, keepdims=True)
    picked = jnp.zeros((table_rows, tokens), jnp.float32)
    mixed = jnp.zeros((table_rows, tokens), jnp.float32)
    for i in range(top):
        hit = ids[i : i + 1, :] == expert_of
        picked = picked + jnp.where(hit, 1.0, 0.0)
        mixed = mixed + jnp.where(hit, mixing[i : i + 1, :], 0.0)
    earlier = lax.broadcasted_iota(jnp.int32, (tokens, tokens), 0) < lax.broadcasted_iota(
        jnp.int32, (tokens, tokens), 1
    )
    rank = jnp.dot(
        picked.astype(jnp.bfloat16),
        jnp.where(earlier, 1.0, 0.0).astype(jnp.bfloat16),
        preferred_element_type=jnp.float32,
    )
    chosen = (picked > 0.5) & (rank.astype(jnp.int32) == place_of)
    dispatch = jnp.where(chosen, 1.0, 0.0).astype(jnp.bfloat16)
    combine = jnp.where(chosen, mixed, 0.0)
    piece_row = lax.rem(lax.broadcasted_iota(jnp.int32, (table_rows, seg), 0), SEGS)
    outgoing = jnp.zeros((table_rows, seg), jnp.float32)
    for s in range(SEGS):
        part = jnp.dot(
            dispatch, tok_ref[:, s * seg : (s + 1) * seg], preferred_element_type=jnp.float32
        )
        outgoing = jnp.where(piece_row == s, part, outgoing)
    send_buf[...] = outgoing.astype(jnp.bfloat16).reshape(send_buf.shape)
    arrived[me] = send_buf[e]

    each_peer(lambda p: token_copy(p, me).start())
    changed = swap_ref[e] != e

    def forward(k):
        copy = to_partner(k)
        copy.wait_recv()
        to_group(k, g).start()
        copy.wait_send()
        if k + WINDOW < pieces:
            to_partner(k + WINDOW).start()

    def choose(k, which):
        k = pieces - 1 - k
        shape = (gu_rows, hid) if k < GU_PIECES else (TILE_ROWS, width)
        took = jnp.broadcast_to(jnp.where(changed, 1, 0), shape) == 1
        if k < GU_PIECES:
            rows = pl.ds(k * gu_rows, gu_rows)
            new = sgu_ref[0, which, rows].astype(jnp.float32)
            old = gu_vmem[which, rows].astype(jnp.float32)
            sgu_ref[0, which, rows] = jnp.where(took, new, old).astype(jnp.bfloat16)
        else:
            start = which * dn_half + (k - GU_PIECES) * TILE_ROWS
            rows = pl.ds(pl.multiple_of(start, TILE_ROWS), TILE_ROWS)
            new = sdn_ref[0, rows].astype(jnp.float32)
            old = dn_vmem[rows].astype(jnp.float32)
            sdn_ref[0, rows] = jnp.where(took, new, old).astype(jnp.bfloat16)

    def settle(k):
        to_group(k, g).wait_send()
        choose(k, g)
        to_group(k, other).wait_recv()
        choose(k, other)

    for k in range(early):
        forward(k)
    for load in loads:
        load.wait()
    each_peer(lambda p: token_copy(p, p).wait_recv())

    block = min(256, peers * TILE_ROWS)
    groups = block // TILE_ROWS

    def expert_block(b, carry):
        start = pl.multiple_of(b * groups, groups)
        rows_in = arrived[pl.ds(start, groups)].reshape(block, seg)
        piece = lax.rem(lax.broadcasted_iota(jnp.int32, (block, hid), 0), SEGS)
        for half_of in range(2):
            total = jnp.zeros((block, hid), jnp.float32)
            for s in range(SEGS):
                part = jnp.dot(
                    rows_in,
                    gu_vmem[half_of, s * seg : (s + 1) * seg, :],
                    preferred_element_type=jnp.float32,
                )
                total = total + jnp.where(piece == s, part, 0.0)
            acc[half_of] = jnp.sum(total.reshape(block // SEGS, SEGS, hid), axis=1)
        gate = acc[0] * width ** (-0.5)
        up = acc[1] * width ** (-0.5)
        hidden = gate / (1.0 + jnp.exp(-gate)) * up
        spread = jnp.broadcast_to(hidden[:, None, :], (block // SEGS, SEGS, hid))
        spread = spread.reshape(block, hid).astype(jnp.bfloat16)
        out_piece = lax.rem(lax.broadcasted_iota(jnp.int32, (block, seg), 0), SEGS)
        for s in range(SEGS):
            part = jnp.dot(
                spread,
                dn_vmem[:, s * seg : (s + 1) * seg],
                preferred_element_type=jnp.float32,
            )
            down_acc[...] = part if s == 0 else jnp.where(out_piece == s, part, down_acc[...])
        scaled = down_acc[...] * (hid * n_dp) ** (-0.5)
        out_buf[pl.ds(start, groups)] = scaled.astype(jnp.bfloat16).reshape(groups, TILE_ROWS, seg)
        return carry

    lax.fori_loop(0, peers * TILE_ROWS // block, expert_block, 0)
    returned[me] = out_buf[me]
    each_peer(lambda p: return_copy(p, me).start())

    for k in range(early - LAG):
        settle(k)
    for k in range(early, late):
        forward(k)
        settle(k - LAG)

    each_peer(lambda p: return_copy(p, p).wait_recv())
    for j in range(n_expert):
        total = returned[j * n_dp].astype(jnp.float32)
        for i in range(1, n_dp):
            total = total + returned[j * n_dp + i].astype(jnp.float32)
        sums[j * TILE_ROWS : (j + 1) * TILE_ROWS, :] = total
    weights = combine.T
    column = lax.rem(lax.broadcasted_iota(jnp.int32, (tokens, table_rows), 1), SEGS)
    for s in range(SEGS):
        moe = jnp.dot(
            jnp.where(column == s, weights, 0.0),
            sums[...],
            precision=lax.Precision.HIGHEST,
            preferred_element_type=jnp.float32,
        )
        moe_ref[:, s * seg : (s + 1) * seg] = moe.astype(jnp.bfloat16)

    for k in range(late, pieces):
        forward(k)
        settle(k - LAG)

    each_peer(lambda p: token_copy(p, p).wait_send())
    each_peer(lambda p: return_copy(p, p).wait_send())
    for k in range(pieces - LAG, pieces):
        settle(k)


def exchange(n_expert, n_dp, expert_ids, affinity, swap_partner, tokens, gate_up, down_proj):
    rows, width = tokens.shape
    hid = gate_up.shape[3]
    peers = n_expert * n_dp
    seg = width * CAP // TILE_ROWS
    block = min(256, peers * TILE_ROWS)
    pieces = GU_PIECES + hid // 2 // TILE_ROWS
    vmem = pl.BlockSpec(memory_space=pltpu.VMEM)
    hbm = pl.BlockSpec(memory_space=pltpu.HBM)
    return pl.pallas_call(
        functools.partial(kernel, n_expert, n_dp),
        out_shape=(
            pltpu.VMEM(gate_up.shape, jnp.bfloat16),
            pltpu.VMEM(down_proj.shape, jnp.bfloat16),
            pltpu.VMEM(tokens.shape, jnp.bfloat16),
        ),
        in_specs=[hbm] * 6,
        out_specs=(vmem, vmem, vmem),
        scratch_shapes=[
            pltpu.VMEM(expert_ids.shape[::-1], jnp.int32),
            pltpu.VMEM(affinity.shape[::-1], jnp.float32),
            pltpu.SMEM(swap_partner.shape, jnp.int32),
            pltpu.VMEM(tokens.shape, jnp.bfloat16),
            pltpu.VMEM((n_expert, TILE_ROWS, seg), jnp.bfloat16),
            pltpu.VMEM((peers, TILE_ROWS, seg), jnp.bfloat16),
            pltpu.VMEM((peers, TILE_ROWS, seg), jnp.bfloat16),
            pltpu.VMEM((peers, TILE_ROWS, seg), jnp.bfloat16),
            pltpu.VMEM((2, block // SEGS, hid), jnp.float32),
            pltpu.VMEM((block, seg), jnp.float32),
            pltpu.VMEM((n_expert * TILE_ROWS, seg), jnp.float32),
            pltpu.VMEM(gate_up.shape[1:], jnp.bfloat16),
            pltpu.VMEM(down_proj.shape[1:], jnp.bfloat16),
            pltpu.SemaphoreType.DMA((6,)),
            pltpu.SemaphoreType.DMA((peers,)),
            pltpu.SemaphoreType.DMA((peers,)),
            pltpu.SemaphoreType.DMA((peers,)),
            pltpu.SemaphoreType.DMA((peers,)),
            pltpu.SemaphoreType.DMA((pieces,)),
            pltpu.SemaphoreType.DMA((pieces,)),
            pltpu.SemaphoreType.DMA((pieces,)),
            pltpu.SemaphoreType.DMA((pieces,)),
        ],
        compiler_params=pltpu.CompilerParams(
            collective_id=0, has_side_effects=True, vmem_limit_bytes=52 * 2**20
        ),
        cost_estimate=pl.CostEstimate(
            flops=2 * peers * TILE_ROWS * 3 * hid * width,
            bytes_accessed=8 * hid * width * 3,
            transcendentals=peers * CAP * hid,
        ),
    )(expert_ids.T, affinity.T, swap_partner, tokens, gate_up, down_proj)


def per_device(n_expert, n_dp, tokens, affinity, expert_ids, swap_partner, gate_up, down_proj):
    new_gate_up, new_down, moe_out = exchange(
        n_expert, n_dp, expert_ids, affinity, swap_partner, tokens, gate_up, down_proj
    )
    return (moe_out, new_gate_up, new_down)


def solution(mesh):
    placed = (
        P(("group", "expert", "dp"), None),
        P(("group", "expert", "dp"), None),
        P(("group", "expert", "dp"), None),
        P("group"),
        P("expert", None, None, "dp"),
        P("expert", "dp", None),
    )
    return jax.shard_map(
        functools.partial(per_device, mesh.shape["expert"], mesh.shape["dp"]),
        mesh=mesh,
        in_specs=placed,
        out_specs=(
            P(("group", "expert", "dp"), None),
            P(("group", "expert"), None, None, "dp"),
            P(("group", "expert"), "dp", None),
        ),
        check_vma=False,
    )
```
